512 devices in a mesh: leaf: 256 (over x, z, y), tile: 2 (over core).
Axes of the slice: x: 4, y: 8, z: 8, core: 2. Of those that a mesh axis runs over, the one named last changes fastest.
Arguments:
- margin_diag: float32 [65536, 256], P('leaf', 'tile'), may hold values from -0.05 to 1.05, as said below
- coupling_near: float32 [65536, 256], P('leaf', 'tile'), may hold values from -0.07 to 0.07
- coupling_far: float32 [65536, 256], P('leaf', 'tile'), may hold values from -0.07 to 0.07
- leaf_factor: float32 [65536, 256], P('leaf', 'tile')
- tile_rows: int32 [256, 2, 4], P('leaf'), may hold values from 0 to 255, as said below
- tile_counts: int32 [256, 2], P('leaf'), may hold values from 1 to 4, as said below
Outputs:
- factor: float32 [1024, 65536], P(None, ('leaf', 'tile'))
The draws below stay inside these ranges and needn't reach their ends.
Inputs may be any that keep to these rules, and one draw needn't show every extreme that they name: Each row block of margin_diag is a symmetric 256 x 256 tile, as an margin tile is. `tile_rows`: every entry names a leaf of the column leaf's group of four. Entry 0 of each list is the leaf itself; at level 0 entry 1 is its sibling i XOR a, and further entries are padding; at level 1 entries 1 to 3 are the other three group members in some order. Entries past the count are padding. `tile_counts`: level 0 counts are 1 or 2, level 1 counts 1 to 4; in every draw some leaf has a full list at each level.
All inputs are finite; a program needn't handle non-finite values.
Results may differ from the reference program's by a relative error of at most 0.0003.
Values sent between devices are 32-bit elements; how exact they have to be, the bound alone decides.
A program may use at most 64 MiB of HBM per device.

```python
import jax
import jax.numpy as jnp
import numpy as np
from jax import lax

ORB = 256
ITERS = 2
ORBITALS = 65536
N_LEAF = 256


def sym_part(key, width, power):
    leaves = ORBITALS // ORB
    uniform_part = jax.random.uniform(key, (leaves, ORB, ORB), jnp.float32, -1.0, 1.0)
    shaped = jnp.sign(uniform_part) * jnp.abs(uniform_part) ** power
    return width * 0.7071 * (shaped + jnp.swapaxes(shaped, 1, 2))


def tile_lists(key):
    leaves = ORBITALS // ORB
    stride = leaves // 4
    leaf_ids = jnp.arange(leaves, dtype=jnp.int32)
    keys = jax.random.split(key, 6)
    count_near = jax.random.randint(keys[0], (leaves,), 1, 3)
    full_near = jax.random.randint(keys[1], (), 0, leaves)
    count_near = jnp.where(leaf_ids == full_near, 2, count_near)
    count_far = jax.random.randint(keys[2], (leaves,), 1, 5)
    full_far = jax.random.randint(keys[3], (), 0, leaves)
    count_far = jnp.where(leaf_ids == full_far, 4, count_far)
    padding = jax.random.randint(keys[4], (leaves, 2), 0, 4) * stride
    near_list = jnp.stack([leaf_ids, jnp.bitwise_xor(leaf_ids, stride), jnp.bitwise_xor(leaf_ids, padding[:, 0]), jnp.bitwise_xor(leaf_ids, padding[:, 1])], axis=1)
    scores = jax.random.randint(keys[5], (leaves, 3), 0, 1 << 20) * 4 + jnp.arange(3, dtype=jnp.int32)[None, :]
    ranking = jnp.argsort(scores, axis=1)
    codes = (jnp.array([1, 2, 3], dtype=jnp.int32) * stride)[ranking]
    far_list = jnp.concatenate([leaf_ids[:, None], jnp.bitwise_xor(leaf_ids[:, None], codes)], axis=1)
    listed = jnp.stack([near_list, far_list], axis=1).astype(jnp.int32)
    counts = jnp.stack([count_near, count_far], axis=1).astype(jnp.int32)
    return (listed, counts)


def draw_margin_diag(key, part):
    shared = sym_part(key, 0.02, 1.0)
    identity = jnp.eye(ORB, dtype=jnp.float32)
    return (identity[None] + shared).reshape(ORBITALS, ORB)


def draw_leaf_factor(key, part):
    shared = sym_part(key, 0.02, 1.0)
    key = jax.random.fold_in(key, 7)
    leaves = ORBITALS // ORB
    noise = 0.006 * jax.random.normal(key, (leaves, ORB, ORB), jnp.float32)
    identity = jnp.eye(ORB, dtype=jnp.float32)
    return (identity[None] - 0.5 * shared + noise).reshape(ORBITALS, ORB)


def draw_tile_rows(key, part):
    listed, counts = tile_lists(key)
    return listed


def draw_tile_counts(key, part):
    listed, counts = tile_lists(key)
    return counts


def levels(key, dims, cuts, least, largest):
    gain = 1.0
    for position, shards_of in cuts:
        steps = jax.random.uniform(jax.random.fold_in(jax.random.fold_in(key, 6), position), (shards_of,), jnp.float32, least / len(cuts), largest / len(cuts))
        gain = gain * jnp.repeat(jnp.exp(steps), dims[position] // shards_of).reshape((-1,) + (1,) * (len(dims) - 1 - position))
    return gain


def centred(key, extent, deviation, reach, cuts=(), held_as=jnp.bfloat16):
    drawn = deviation * jax.random.normal(key, extent, jnp.float32)
    if cuts:
        drawn = drawn * levels(key, extent, cuts, -0.22, 0.18)
    return jnp.clip(drawn, -reach, reach).astype(held_as)


def setup_inputs(seed: int = 0) -> dict:
    streams_of = jax.random.split(jax.random.key(seed), 7)
    return {
        "margin_diag": draw_margin_diag(jax.random.fold_in(streams_of[6], 71), 0),
        "coupling_near": centred(streams_of[1], (ORBITALS, ORB), 0.012, 0.07, ((0, 256), (1, 2)), jnp.float32),
        "coupling_far": centred(streams_of[2], (ORBITALS, ORB), 0.012, 0.07, ((0, 256), (1, 2)), jnp.float32),
        "leaf_factor": draw_leaf_factor(jax.random.fold_in(streams_of[6], 71), 0),
        "tile_rows": draw_tile_rows(jax.random.fold_in(streams_of[6], 71), 0),
        "tile_counts": draw_tile_counts(jax.random.fold_in(streams_of[6], 71), 0),
    }


flip_near = np.array([1, 0, 3, 2])
flip_far = np.array([2, 3, 0, 1])
highest = lax.Precision.HIGHEST


def reference(margin_diag, coupling_near, coupling_far, leaf_factor, tile_rows, tile_counts):
    stride = N_LEAF // 4

    def quads(values):
        tail = values.shape[1:]
        order = (2, 0, 1) + tuple(range(3, 3 + len(tail)))
        return values.reshape((2, 2, stride) + tail).transpose(order).reshape((stride, 4) + tail)

    def blocks(values):
        return quads(values.reshape(N_LEAF, ORB, ORB))

    positions = jnp.arange(4)
    identity = jnp.eye(ORB, dtype=jnp.float32)
    unit_four = jnp.eye(4, dtype=jnp.float32)

    def one_quad(quad_data):
        diag_rows, near_raw, far_raw, starts, listed, live_count = quad_data
        near_rows = 0.5 * (near_raw + jnp.swapaxes(near_raw[flip_near], 1, 2))
        far_rows = 0.5 * (far_raw + jnp.swapaxes(far_raw[flip_far], 1, 2))
        factor = jnp.zeros((4, 4, ORB, ORB), jnp.float32).at[positions, positions].set(starts)
        for tree_level in range(2):
            where_rows = listed[:, tree_level, :]
            slot_pos = 2 * ((where_rows // (2 * stride)) % 2) + (where_rows // stride) % 2
            is_live = positions[None, :] < live_count[:, tree_level][:, None]
            row_mask = jnp.any(is_live[:, :, None] & (slot_pos[:, :, None] == positions[None, None, :]), axis=1).astype(jnp.float32)
            for iteration in range(ITERS):
                applied = jnp.einsum('rab,jrbc->jrac', diag_rows, factor, precision=highest)
                applied = applied + jnp.einsum('rab,jrbc->jrac', near_rows, factor[:, flip_near], precision=highest)
                if tree_level == 1:
                    applied = applied + jnp.einsum('rab,jrbc->jrac', far_rows, factor[:, flip_far], precision=highest)
                gram = jnp.einsum('lrak,jrac->ljkc', factor, applied, precision=highest)
                residual_gram = unit_four[:, :, None, None] * identity - gram
                factor = factor + 0.5 * jnp.einsum('lrak,ljkc->jrac', factor, residual_gram, precision=highest)
                factor = factor * row_mask[:, :, None, None]
        return factor

    joined = lax.map(one_quad, (blocks(margin_diag), blocks(coupling_near), blocks(coupling_far), blocks(leaf_factor), quads(tile_rows), quads(tile_counts)))
    joined = joined.reshape(stride, 2, 2, 4, ORB, ORB).transpose(1, 2, 0, 3, 4, 5)
    joined = joined.reshape(N_LEAF, 4 * ORB, ORB).transpose(1, 0, 2)
    return joined.reshape(4 * ORB, N_LEAF * ORB)
```

```python
import functools

import jax
import jax.numpy as jnp
from jax import lax
from jax.experimental import pallas as pl
from jax.experimental.pallas import tpu as pltpu

MESH = pl.DeviceIdType.MESH
T = 256
H = 128
F32 = jnp.float32
BF16 = jnp.bfloat16


def split(x):
    high = x.astype(BF16)
    return high, (x - high.astype(F32)).astype(BF16)


def nn(a, b):
    return lax.dot_general(a, b, (((1,), (0,)), ((), ())), preferred_element_type=F32)


def nt(a, b):
    return lax.dot_general(a, b, (((1,), (1,)), ((), ())), preferred_element_type=F32)


def mm(a, b, dot=nn):
    rows = a[0].shape[0]
    if rows <= 128:
        both = dot(jnp.concatenate([a[0], a[1]], 0), b[0])
        return both[:rows] + (both[rows:] + dot(a[0], b[1]))
    return dot(a[0], b[0]) + (dot(a[0], b[1]) + dot(a[1], b[0]))


def put(pair_ref, index, value):
    high, low = split(value)
    pair_ref[(0,) + index] = high
    pair_ref[(1,) + index] = low


def get(pair_ref, index):
    return pair_ref[(0,) + index], pair_ref[(1,) + index]


ALL = slice(None)


def tl(k):
    return slice(k * T, (k + 1) * T)


def eye(offset, rows):
    row = lax.broadcasted_iota(jnp.int32, (rows, T), 0) + offset
    col = lax.broadcasted_iota(jnp.int32, (rows, T), 1)
    return jnp.where(row == col, 1.0, 0.0).astype(F32)


def kernel(
    stride,
    diag_ref, near_ref, far_ref, leaf_ref, rows_ref, counts_ref,
    out_ref,
    raw, uraw, masks, mown,
    ut, a_mat, far_s, p_mat, v_mat, f_mat, f_cross,
    xs, xr, ms, mr, ds, dr,
):
    leaf = lax.axis_index("leaf")
    core = lax.axis_index("tile")
    pos = leaf // stride
    rest = leaf % stride
    pos1 = pos + 1 - 2 * (pos % 2)
    pos2 = (pos + 2) % 4
    pos3 = 3 - pos
    spot = (pos, pos1, pos2, pos3)
    dev1 = (pos1 * stride + rest, core)
    dev2 = (pos2 * stride + rest, core)
    dev3 = (pos3 * stride + rest, core)
    mate = (leaf, 1 - core)
    half = core * H

    raw[0, 0, core] = diag_ref[...]
    raw[1, 0, core] = near_ref[...]
    raw[2, 0, core] = far_ref[...]
    uraw[0, core] = leaf_ref[...].T
    for level in range(2):
        for s in range(4):
            hit = jnp.float32(0.0)
            for e in range(4):
                value = rows_ref[0, level, e]
                place = 2 * (value // (2 * stride) % 2) + value // stride % 2
                live = jnp.logical_and(e < counts_ref[0, level], place == spot[s])
                hit = jnp.where(live, jnp.float32(1.0), hit)
            mown[pl.ds(level * 4 + s, 1), :] = jnp.full((1, 128), hit, F32)

    barrier = pltpu.get_barrier_semaphore()
    for device in (dev1, dev2, dev3, mate):
        pl.semaphore_signal(barrier, inc=1, device_id=device, device_id_type=MESH)
    pl.semaphore_wait(barrier, 4)

    def tile_ref(kind, slot, side, piece):
        if kind == 3:
            if piece is None:
                return uraw.at[slot, side]
            return uraw.at[slot, side, pl.ds(piece * 64, 64)]
        if piece is None:
            return raw.at[kind, slot, side]
        return raw.at[kind, slot, side, pl.ds(piece * H, H)]

    def to_chip(kind, src_slot, piece, dst_slot, device, sem):
        return pltpu.make_async_remote_copy(
            src_ref=tile_ref(kind, src_slot, core, piece),
            dst_ref=tile_ref(kind, dst_slot, core, piece),
            send_sem=xs.at[kind, sem], recv_sem=xr.at[kind, sem],
            device_id=device, device_id_type=MESH,
        )

    def to_mate(kind, slot, piece, sem):
        return pltpu.make_async_remote_copy(
            src_ref=tile_ref(kind, slot, core, piece),
            dst_ref=tile_ref(kind, slot, core, piece),
            send_sem=ds.at[kind, sem], recv_sem=dr.at[kind, sem],
            device_id=mate, device_id_type=MESH,
        )

    def own1(kind):
        return to_chip(kind, 0, None, 1, dev1, 0)

    def own3(kind):
        return to_chip(kind, 0, None, 3, dev3, 1)

    def fwd1(kind):
        return to_chip(kind, 3, 0, 2, dev1, 2)

    def fwd3(kind):
        return to_chip(kind, 1, 1, 2, dev3, 3)

    def masks_to(slot, device):
        return pltpu.make_async_remote_copy(
            src_ref=mown, dst_ref=masks.at[slot],
            send_sem=ms.at[slot], recv_sem=mr.at[slot],
            device_id=device, device_id_type=MESH,
        )

    mask_copies = [masks_to(1, dev1), masks_to(2, dev2), masks_to(3, dev3)]
    for copy in mask_copies:
        copy.start()
    for kind in (1, 3, 0):
        own1(kind).start()
        own3(kind).start()
    for kind in (3, 0, 1, 2):
        to_mate(kind, 0, None, 0).start()

    def hop(kind):
        own1(kind).wait_recv()
        to_mate(kind, 1, None, 1).start()
        fwd3(kind).start()
        own3(kind).wait_recv()
        to_mate(kind, 3, None, 3).start()
        fwd1(kind).start()

    def hop2(kind):
        fwd1(kind).wait_recv()
        to_mate(kind, 2, 0, 2).start()
        fwd3(kind).wait_recv()
        to_mate(kind, 2, 1, 4).start()

    def mate_in(kind, slot):
        if slot == 2:
            to_mate(kind, 2, 0, 2).wait_recv()
            to_mate(kind, 2, 1, 4).wait_recv()
        else:
            to_mate(kind, slot, None, slot).wait_recv()

    for kind in (1, 3, 0):
        hop(kind)
    own1(2).start()
    own3(2).start()

    for copy in mask_copies:
        copy.wait_recv()
    masks[0] = mown[...]

    def mask(level, column, row):
        line = masks[column, pl.ds(level * 4 + (column ^ row), 1), :]
        return jnp.concatenate([line, line], axis=1)

    def whole(kind, slot):
        return jnp.concatenate([raw[kind, slot, 0], raw[kind, slot, 1]], axis=1)

    def pair(g):
        s0, s1 = 2 * g, 2 * g + 1
        for k, slot in enumerate((s0, s1)):
            put(a_mat, (g, tl(k), tl(k)), whole(0, slot))
            put(ut, (slot,), jnp.concatenate([uraw[slot, 0], uraw[slot, 1]], axis=0))
        first = whole(1, s0)
        second = whole(1, s1)
        cross = 0.5 * (first + second.T)
        put(a_mat, (g, tl(0), tl(1)), cross)
        put(a_mat, (g, tl(1), tl(0)), cross.T)
        one = eye(0, T)
        for j in range(2):
            v = split(mm(get(ut, (2 * g + j,)), get(a_mat, (g, tl(j), ALL))))
            for r in range(2):
                gram = mm((v[0][:, tl(r)], v[1][:, tl(r)]), get(ut, (2 * g + r,)), nt)
                f = -0.5 * gram
                if r == j:
                    f = f + 1.5 * one
                new = mm(split(f), get(ut, (2 * g + r,)))
                new = new * mask(0, 2 * g + j, 2 * g + r)
                put(p_mat, (g, tl(j), tl(r)), new)

        def gram_of():
            put(v_mat, (), mm(get(p_mat, (g,)), get(a_mat, (g,))))
            gram = mm(get(v_mat, ()), get(p_mat, (g,)), nt)
            for j in range(2):
                for r in range(2):
                    f = -0.5 * gram[tl(j), tl(r)]
                    if r == j:
                        f = f + 1.5 * one
                    put(f_mat, (g, tl(j), tl(r)), f)

        gram_of()
        new = mm(get(f_mat, (g,)), get(p_mat, (g,)))
        for j in range(2):
            for r in range(2):
                put(p_mat, (g, tl(j), tl(r)), new[tl(j), tl(r)] * mask(0, 2 * g + j, 2 * g + r))
        gram_of()

    for slot in (0, 1):
        for kind in (0, 1, 3):
            mate_in(kind, slot)
    pair(0)
    for kind in (1, 3, 0):
        hop2(kind)
    hop(2)
    for slot in (2, 3):
        for kind in (0, 1, 3):
            mate_in(kind, slot)
    pair(1)
    hop2(2)
    for slot in range(4):
        mate_in(2, slot)
    for k in range(2):
        put(far_s, (k,), 0.5 * (whole(2, k) + whole(2, k + 2).T))

    for k in range(2):
        put(v_mat, (ALL, tl(k)), mm(get(p_mat, (0, ALL, tl(k))), get(far_s, (k,))))
    put(f_cross, (), -0.5 * mm(get(v_mat, ()), get(p_mat, (1,)), nt))

    mine = pl.ds(pl.multiple_of(half, H), H)
    u0 = mm(get(f_mat, (0, mine, ALL)), get(p_mat, (0,)))
    u1 = mm(get(f_cross, (mine, ALL)), get(p_mat, (1,)))
    u = [u0[:, tl(0)], u0[:, tl(1)], u1[:, tl(0)], u1[:, tl(1)]]
    u = [u[r] * mask(1, 0, r) for r in range(4)]
    us = [split(x) for x in u]

    def beside(parts):
        return tuple(jnp.concatenate([part[i] for part in parts], axis=1) for i in range(2))

    v = []
    for g in range(2):
        vg = mm(beside(us[2 * g:2 * g + 2]), get(a_mat, (g,)))
        for k in range(2):
            extra = mm(us[2 - 2 * g + k], get(far_s, (k,)), nn if g == 1 else nt)
            v.append(split(vg[:, tl(k)] + extra))
    ga = [mm(v[r], get(p_mat, (r // 2, ALL, tl(r % 2))), nt) for r in range(4)]
    terms = [[None] * 4, [None] * 4]
    for l in range(4):
        lhs = []
        for g in range(2):
            m0, m1 = mask(1, l, 2 * g), mask(1, l, 2 * g + 1)
            m0, m1 = jnp.concatenate([m0, m0], 1), jnp.concatenate([m1, m1], 1)
            lhs.append(split(m0 * ga[2 * g] + m1 * ga[2 * g + 1]))
        k = l % 2
        if l < 2:
            gram = mm(lhs[0], get(f_mat, (0, ALL, tl(k)))) + mm(lhs[1], get(f_cross, (tl(k), ALL)), nt)
        else:
            gram = mm(lhs[0], get(f_cross, (ALL, tl(k)))) + mm(lhs[1], get(f_mat, (1, ALL, tl(k))))
        d = -gram
        if l == 0:
            d = d + eye(half, H)
        d = split(d)
        if l < 2:
            terms[0][l] = mm(d, get(f_mat, (0, tl(k), ALL)))
            terms[1][l] = mm(d, get(f_cross, (tl(k), ALL)))
        else:
            terms[0][l] = mm(d, get(f_cross, (ALL, tl(k))), nt)
            terms[1][l] = mm(d, get(f_mat, (1, tl(k), ALL)))
    for r in range(4):
        g, k = r // 2, r % 2
        x = 0.0
        for l in range(4):
            line = mask(1, l, r)
            x = x + jnp.concatenate([line, line], 1) * terms[g][l]
        last = u[r] + 0.5 * mm(split(x), get(p_mat, (g, ALL, tl(k))))
        last = last * mask(1, 0, r)
        out_ref[pl.ds(pl.multiple_of(spot[r] * T, T), T), :] = last.T

    for copy in mask_copies:
        copy.wait_send()
    for kind in range(4):
        for copy in (own1(kind), own3(kind), fwd1(kind), fwd3(kind)):
            copy.wait_send()
        to_mate(kind, 0, None, 0).wait_send()
        to_mate(kind, 1, None, 1).wait_send()
        to_mate(kind, 3, None, 3).wait_send()
        to_mate(kind, 2, 0, 2).wait_send()
        to_mate(kind, 2, 1, 4).wait_send()


def per_device(margin_diag, coupling_near, coupling_far, leaf_factor, tile_rows, tile_counts):
    stride = lax.axis_size("leaf") // 4
    vmem = pl.BlockSpec(memory_space=pltpu.VMEM)
    smem = pl.BlockSpec(memory_space=pltpu.SMEM)
    dma = pltpu.SemaphoreType.DMA
    return pl.pallas_call(
        functools.partial(kernel, stride),
        out_shape=jax.ShapeDtypeStruct((4 * T, H), F32),
        in_specs=[vmem] * 4 + [smem] * 2,
        out_specs=vmem,
        scratch_shapes=[
            pltpu.VMEM((3, 4, 2, T, H), F32),
            pltpu.VMEM((4, 2, H, T), F32),
            pltpu.VMEM((4, 8, 128), F32),
            pltpu.VMEM((8, 128), F32),
            pltpu.VMEM((2, 4, T, T), BF16),
            pltpu.VMEM((2, 2, 2 * T, 2 * T), BF16),
            pltpu.VMEM((2, 2, T, T), BF16),
            pltpu.VMEM((2, 2, 2 * T, 2 * T), BF16),
            pltpu.VMEM((2, 2 * T, 2 * T), BF16),
            pltpu.VMEM((2, 2, 2 * T, 2 * T), BF16),
            pltpu.VMEM((2, 2 * T, 2 * T), BF16),
            dma((4, 4)), dma((4, 4)), dma((4,)), dma((4,)), dma((4, 5)), dma((4, 5)),
        ],
        compiler_params=pltpu.CompilerParams(
            collective_id=0, has_side_effects=True, vmem_limit_bytes=50 * 2**20
        ),
    )(margin_diag, coupling_near, coupling_far, leaf_factor, tile_rows, tile_counts)


def solution(mesh):
    spec = jax.sharding.PartitionSpec
    return jax.shard_map(
        per_device,
        mesh=mesh,
        in_specs=(
            spec("leaf", "tile"),
            spec("leaf", "tile"),
            spec("leaf", "tile"),
            spec("leaf", "tile"),
            spec("leaf", None, None),
            spec("leaf", None),
        ),
        out_specs=spec(None, ("leaf", "tile")),
        check_vma=False,
    )
```

```python
import functools

import jax
import jax.numpy as jnp
from jax import lax
from jax.experimental import pallas as pl
from jax.experimental.pallas import tpu as pltpu

MESH = pl.DeviceIdType.MESH
T = 256
H = 128
KP = 96
F32 = jnp.float32
BF16 = jnp.bfloat16


def split(x):
    high = x.astype(BF16)
    return high, (x - high.astype(F32)).astype(BF16)


def nn(a, b):
    return lax.dot_general(a, b, (((1,), (0,)), ((), ())), preferred_element_type=F32)


def nt(a, b):
    return lax.dot_general(a, b, (((1,), (1,)), ((), ())), preferred_element_type=F32)


def mm(a, b, dot=nn):
    rows = a[0].shape[0]
    if rows <= 128:
        both = dot(jnp.concatenate([a[0], a[1]], 0), b[0])
        return both[:rows] + (both[rows:] + dot(a[0], b[1]))
    return dot(a[0], b[0]) + (dot(a[0], b[1]) + dot(a[1], b[0]))


def put(pair_ref, index, value):
    high, low = split(value)
    pair_ref[(0,) + index] = high
    pair_ref[(1,) + index] = low


def get(pair_ref, index):
    return pair_ref[(0,) + index], pair_ref[(1,) + index]


ALL = slice(None)


def tl(k):
    return slice(k * T, (k + 1) * T)


def eye(offset, rows):
    row = lax.broadcasted_iota(jnp.int32, (rows, T), 0) + offset
    col = lax.broadcasted_iota(jnp.int32, (rows, T), 1)
    return jnp.where(row == col, 1.0, 0.0).astype(F32)


def kernel(
    stride,
    diag_ref, near_ref, far_ref, leaf_ref, rows_ref, counts_ref,
    out_ref,
    zin, rows_s, counts_s, own_diag, c_raw, c_own, d_raw, uraw, packed, ncr, masks, mown,
    pf, ff, fx, ut, a_mat, far_s, p_mat, q_mat, f_mat, f_cross,
    local, ssem, rsem,
):
    leaf = lax.axis_index("leaf")
    core = lax.axis_index("tile")
    pos = leaf // stride
    rest = leaf % stride
    pos1 = pos + 1 - 2 * (pos % 2)
    pos2 = (pos + 2) % 4
    pos3 = 3 - pos
    spot = (pos, pos1, pos2, pos3)
    dev1 = (pos1 * stride + rest, core)
    dev3 = (pos3 * stride + rest, core)
    mate = (leaf, 1 - core)
    half = pl.multiple_of(core * H, H)
    mine = pl.ds(half, H)
    away = pl.ds(pl.multiple_of(H - half, H), H)

    barrier = pltpu.get_barrier_semaphore()
    for device in (dev1, dev3, mate):
        pl.semaphore_signal(barrier, inc=1, device_id=device, device_id_type=MESH)

    loads = [
        pltpu.make_async_copy(a, b, local.at[i])
        for i, (a, b) in enumerate((
            (leaf_ref, zin), (near_ref, c_raw.at[0, core]), (diag_ref, own_diag.at[core]),
            (far_ref, d_raw.at[0, core]), (rows_ref, rows_s), (counts_ref, counts_s),
        ))
    ]
    for load in loads:
        load.start()

    copies = {}

    def plan(name, src, dst, device):
        index = len(copies)
        copies[name] = pltpu.make_async_remote_copy(
            src_ref=src, dst_ref=dst, send_sem=ssem.at[index], recv_sem=rsem.at[index],
            device_id=device, device_id_type=MESH,
        )

    def same(name, ref, device):
        plan(name, ref, ref, device)

    def start(*names):
        for name in names:
            copies[name].start()

    def arrived(*names):
        for name in names:
            copies[name].wait_recv()

    plan("C1", c_raw.at[0, core], c_raw.at[1, core], dev1)
    for key, buf, rows in (("U", uraw, 64), ("K", packed, KP), ("D", d_raw, H)):
        first, second = pl.ds(0, rows), pl.ds(rows, rows)
        plan(key + "1b", buf.at[0, core, second], buf.at[1, core, second], dev1)
        plan(key + "1a", buf.at[0, core, first], buf.at[1, core, first], dev1)
        plan(key + "3a", buf.at[0, core, first], buf.at[3, core, first], dev3)
        plan(key + "3b", buf.at[0, core, second], buf.at[3, core, second], dev3)
        plan("f" + key + "1", buf.at[3, core, first], buf.at[2, core, first], dev1)
        plan("f" + key + "3", buf.at[1, core, second], buf.at[2, core, second], dev3)
        if key != "K":
            same("m" + key + "0", buf.at[0, core], mate)
        same("m" + key + "1", buf.at[1, core], mate)
        same("m" + key + "3", buf.at[3, core], mate)
        same("m" + key + "2a", buf.at[2, core, first], mate)
        same("m" + key + "2b", buf.at[2, core, second], mate)
    plan("mC0", c_raw.at[0, core, away], c_own.at[:], mate)
    same("mR", ncr.at[0, mine], mate)
    same("mG0", own_diag.at[core], mate)
    plan("N3", ncr.at[0, mine], ncr.at[1, mine], dev3)
    same("mN", ncr.at[1, mine], mate)
    plan("M1", mown, masks.at[1], dev1)
    plan("M3", mown, masks.at[3], dev3)
    plan("fM1", masks.at[3], masks.at[2], dev1)
    for g in range(2):
        for r in range(2):
            same("xP%d%d" % (g, r), pf.at[g, core, r], mate)
    for g in range(2):
        same("xF%d" % g, ff.at[g, core], mate)
    same("xX", fx.at[core], mate)

    loads[4].wait()
    loads[5].wait()
    for level in range(2):
        for s in range(4):
            hit = jnp.float32(0.0)
            for e in range(4):
                value = rows_s[0, level, e]
                place = 2 * (value // (2 * stride) % 2) + value // stride % 2
                live = jnp.logical_and(e < counts_s[0, level], place == spot[s])
                hit = jnp.where(live, jnp.float32(1.0), hit)
            mown[level * 4 + s:level * 4 + s + 1, :] = jnp.full((1, 128), hit, F32)
    masks[0] = mown[...]

    loads[0].wait()
    uraw[0, core] = zin[...].T
    loads[1].wait()
    pl.semaphore_wait(barrier, 3)
    start("M1", "M3", "C1", "U3a", "U3b", "U1b", "U1a", "mC0", "mU0")
    loads[2].wait()
    packed[0, core, 0:H] = own_diag[core, pl.ds(half, H)]
    other = own_diag[core, pl.ds(pl.multiple_of(H - half, H), H)]
    other = jnp.where(core == 0, other, other.T)
    packed[0, core, H:H + 64] = jnp.where(core == 0, other[0:64], other[64:128])
    start("K3a", "K3b", "K1b", "K1a", "mG0")
    loads[3].wait()
    start("mD0")
    def mask(level, column, row):
        line = masks[column, level * 4 + (column ^ row):level * 4 + (column ^ row) + 1, :]
        return jnp.concatenate([line, line], axis=1)

    def wide(line):
        return jnp.concatenate([line, line], axis=1)

    def whole(ref, slot):
        return jnp.concatenate([ref[slot, 0], ref[slot, 1]], axis=1)

    def put_near(g, cross):
        first, second = (0, 1) if g == 0 else (1, 0)
        put(a_mat, (g, tl(first), tl(second)), cross)
        put(a_mat, (g, tl(second), tl(first)), cross.T)

    def put_diag(slot):
        g, k = slot // 2, slot % 2
        low, high = packed[slot, 0], packed[slot, 1]
        below = jnp.concatenate([low[H:], high[H:]], axis=0)
        full = jnp.concatenate([
            jnp.concatenate([low[:H], below.T], axis=1),
            jnp.concatenate([below, high[:H]], axis=1),
        ], axis=0)
        put(a_mat, (g, tl(k), tl(k)), full)

    def put_leaf(slot):
        put(ut, (slot,), jnp.concatenate([uraw[slot, 0], uraw[slot, 1]], axis=0))

    own_rows = pl.ds(pl.multiple_of(core * T, T), T)
    mate_rows = pl.ds(pl.multiple_of(T - core * T, T), T)

    def sweep1(g, *places):
        hold = {}

        def one():
            for j, r in places:
                hold[j, r] = split(mm(get(ut, (2 * g + j,)), get(a_mat, (g, tl(j), tl(r)))))

        def two():
            for j, r in places:
                f = -0.5 * mm(hold[j, r], get(ut, (2 * g + r,)), nt)
                hold[j, r] = split(f + 1.5 * eye(0, T) if r == j else f)

        def three():
            for j, r in places:
                new = mm(hold[j, r], get(ut, (2 * g + r,)))
                put(p_mat, (g, tl(j), tl(r)), new * mask(0, 2 * g + j, 2 * g + r))

        return one, two, three

    row2 = lax.broadcasted_iota(jnp.int32, (T, 2 * T), 0) + core * T
    col2 = lax.broadcasted_iota(jnp.int32, (T, 2 * T), 1)

    def newton(gram):
        return jnp.where(row2 == col2, 1.5, 0.0) - 0.5 * gram

    def sweep2(g):
        hold = []

        def one():
            hold.append(split(mm(get(p_mat, (g, own_rows)), get(a_mat, (g,)))))

        def two():
            hold.append(split(newton(mm(hold[0], get(p_mat, (g,)), nt))))

        def three():
            for r in range(2):
                line = masks[2 * g + core, pl.ds(core if r == 0 else 1 - core, 1), :]
                new = mm(hold[1], get(p_mat, (g, ALL, tl(r)))) * wide(line)
                pf[g, core, r] = new
                start("xP%d%d" % (g, r))
                put(q_mat, (g, own_rows, tl(r)), new)

        return one, two, three

    def join(g):
        for r in range(2):
            arrived("xP%d%d" % (g, r))
            put(q_mat, (g, mate_rows, tl(r)), pf[g, 1 - core, r])

    def gram1(g):
        hold = []

        def one():
            hold.append(split(mm(get(q_mat, (g, own_rows)), get(a_mat, (g,)))))

        def two():
            f = newton(mm(hold[0], get(q_mat, (g,)), nt))
            ff[g, core] = f
            start("xF%d" % g)
            put(f_mat, (g, own_rows), f)

        return one, two

    def fin(g):
        arrived("xF%d" % g)
        put(f_mat, (g, mate_rows), ff[g, 1 - core])

    def run(*steps):
        for step in steps:
            step()

    arrived("mC0", "C1")
    mixed = c_raw[0, core, mine]
    rows = jnp.where(core == 0, jnp.concatenate([mixed, c_own[...]], axis=1), jnp.concatenate([c_own[...], mixed], axis=1))
    ncr[0, mine] = 0.5 * (rows + c_raw[1, core].T)
    start("N3", "mR")
    arrived("M3")
    start("fM1")
    arrived("U3a")
    start("fU1")
    arrived("U3b")
    start("mU3")
    arrived("K3a")
    start("fK1", "D1b", "D1a")
    arrived("mG0", "mU0")
    put(a_mat, (0, tl(0), tl(0)), jnp.concatenate([own_diag[0], own_diag[1]], axis=1))
    put_leaf(0)
    arrived("U1b")
    start("fU3")
    arrived("U1a", "K3b")
    start("mU1", "mK3")
    arrived("mR", "M1")
    put_near(0, ncr[0])
    run(*sweep1(0, (0, 0)))
    arrived("K1b")
    start("fK3", "D3a", "D3b")
    arrived("mU1")
    put_leaf(1)
    a = sweep1(0, (0, 1), (1, 0))
    run(a[0])
    arrived("K1a")
    start("mK1")
    run(*a[1:])
    arrived("mU3", "mK3")
    put_leaf(3)
    put_diag(3)
    arrived("fM1")
    arrived("N3")
    start("mN")
    arrived("mK1")
    put_diag(1)
    arrived("fU1")
    start("mU2a")
    a, b = sweep1(0, (1, 1)), sweep1(1, (1, 1))
    run(a[0], b[0], a[1], b[1])
    arrived("fU3")
    start("mU2b")
    run(a[2], b[2])
    a = sweep2(0)
    run(a[0])
    arrived("fK1")
    start("mK2a")
    arrived("mN")
    put_near(1, ncr[1])
    run(a[1])
    arrived("fK3")
    start("mK2b")
    arrived("mU2a", "mU2b")
    put_leaf(2)
    b = sweep1(1, (0, 1), (1, 0))
    run(a[2], b[0], b[1])
    arrived("mK2a", "mK2b")
    put_diag(2)
    a = sweep1(1, (0, 0))
    run(a[0], b[2])
    arrived("D1b")
    start("fD3")
    run(a[1])
    arrived("D3a")
    start("fD1")
    join(0)
    run(a[2])
    arrived("D1a", "D3b")
    start("mD1", "mD3")
    a, b = sweep2(1), gram1(0)
    run(a[0], b[0], a[1], b[1], a[2])
    arrived("mD1", "mD3")
    put(far_s, (1,), 0.5 * (whole(d_raw, 1) + whole(d_raw, 3).T))
    arrived("fD1", "fD3")
    start("mD2a", "mD2b")
    fin(0)
    join(1)
    a = gram1(1)
    run(a[0])
    u0 = mm(get(f_mat, (0, mine, ALL)), get(q_mat, (0,)))
    run(a[1])
    arrived("mD0", "mD2a", "mD2b")
    put(far_s, (0,), 0.5 * (whole(d_raw, 0) + whole(d_raw, 2).T))

    second = pl.ds(pl.multiple_of(T + half, H), H)
    v = []
    for k in range(2):
        rows = tuple(
            jnp.concatenate([q_mat[i, 0, mine, tl(k)], q_mat[i, 0, second, tl(k)]], axis=0)
            for i in range(2)
        )
        v.append(mm(rows, get(far_s, (k,))))
    f = -0.5 * mm(split(jnp.concatenate(v, axis=1)), get(q_mat, (1,)), nt)
    fx[core] = f
    start("xX")
    f = split(f)
    for i in range(2):
        f_cross[i, mine] = f[i][:H]
        f_cross[i, second] = f[i][H:]
    u1 = mm((f[0][:H], f[1][:H]), get(q_mat, (1,)))
    u = [u0[:, tl(0)], u0[:, tl(1)], u1[:, tl(0)], u1[:, tl(1)]]
    u = [u[r] * mask(1, 0, r) for r in range(4)]
    us = [split(x) for x in u]

    def beside(parts):
        return tuple(jnp.concatenate([part[i] for part in parts], axis=1) for i in range(2))

    v = []
    for g in range(2):
        vg = mm(beside(us[2 * g:2 * g + 2]), get(a_mat, (g,)))
        for k in range(2):
            extra = mm(us[2 - 2 * g + k], get(far_s, (k,)), nn if g == 1 else nt)
            v.append(split(vg[:, tl(k)] + extra))
    ga = [mm(v[r], get(q_mat, (r // 2, ALL, tl(r % 2))), nt) for r in range(4)]
    fin(1)
    arrived("xX")
    f = split(fx[1 - core])
    for i in range(2):
        f_cross[i, away] = f[i][:H]
        f_cross[i, pl.ds(pl.multiple_of(T + H - half, H), H)] = f[i][H:]
    ds = []
    for l in range(4):
        lhs = []
        for g in range(2):
            m0, m1 = wide(mask(1, l, 2 * g)), wide(mask(1, l, 2 * g + 1))
            lhs.append(split(m0 * ga[2 * g] + m1 * ga[2 * g + 1]))
        k = l % 2
        if l < 2:
            gram = mm(lhs[0], get(f_mat, (0, ALL, tl(k)))) + mm(lhs[1], get(f_cross, (tl(k), ALL)), nt)
        else:
            gram = mm(lhs[0], get(f_cross, (ALL, tl(k)))) + mm(lhs[1], get(f_mat, (1, ALL, tl(k))))
        ds.append(split(eye(half, H) - gram if l == 0 else -gram))
    terms = [[], []]
    for l in range(4):
        k = l % 2
        if l < 2:
            terms[0].append(mm(ds[l], get(f_mat, (0, tl(k), ALL))))
            terms[1].append(mm(ds[l], get(f_cross, (tl(k), ALL))))
        else:
            terms[0].append(mm(ds[l], get(f_cross, (ALL, tl(k))), nt))
            terms[1].append(mm(ds[l], get(f_mat, (1, tl(k), ALL))))
    for r in range(4):
        g, k = r // 2, r % 2
        x = 0.0
        for l in range(4):
            x = x + wide(mask(1, l, r)) * terms[g][l]
        last = u[r] + 0.5 * mm(split(x), get(q_mat, (g, ALL, tl(k))))
        last = last * mask(1, 0, r)
        out_ref[pl.ds(pl.multiple_of(spot[r] * T, T), T), :] = last.T

    for copy in copies.values():
        copy.wait_send()


def per_device(margin_diag, coupling_near, coupling_far, leaf_factor, tile_rows, tile_counts):
    stride = lax.axis_size("leaf") // 4
    vmem = pl.BlockSpec(memory_space=pltpu.VMEM)
    hbm = pl.BlockSpec(memory_space=pl.ANY)
    dma = pltpu.SemaphoreType.DMA
    return pl.pallas_call(
        functools.partial(kernel, stride),
        out_shape=jax.ShapeDtypeStruct((4 * T, H), F32),
        in_specs=[hbm] * 6,
        out_specs=vmem,
        scratch_shapes=[
            pltpu.VMEM((T, H), F32),
            pltpu.SMEM((1, 2, 4), jnp.int32),
            pltpu.SMEM((1, 2), jnp.int32),
            pltpu.VMEM((2, T, H), F32),
            pltpu.VMEM((2, 2, T, H), F32),
            pltpu.VMEM((H, H), F32),
            pltpu.VMEM((4, 2, T, H), F32),
            pltpu.VMEM((4, 2, H, T), F32),
            pltpu.VMEM((4, 2, 2 * KP, H), F32),
            pltpu.VMEM((2, T, T), F32),
            pltpu.VMEM((4, 8, 128), F32),
            pltpu.VMEM((8, 128), F32),
            pltpu.VMEM((2, 2, 2, T, T), F32),
            pltpu.VMEM((2, 2, T, 2 * T), F32),
            pltpu.VMEM((2, T, 2 * T), F32),
            pltpu.VMEM((2, 4, T, T), BF16),
            pltpu.VMEM((2, 2, 2 * T, 2 * T), BF16),
            pltpu.VMEM((2, 2, T, T), BF16),
            pltpu.VMEM((2, 2, 2 * T, 2 * T), BF16),
            pltpu.VMEM((2, 2, 2 * T, 2 * T), BF16),
            pltpu.VMEM((2, 2, 2 * T, 2 * T), BF16),
            pltpu.VMEM((2, 2 * T, 2 * T), BF16),
            dma((6,)), dma((64,)), dma((64,)),
        ],
        compiler_params=pltpu.CompilerParams(
            collective_id=0, has_side_effects=True, vmem_limit_bytes=50 * 2**20
        ),
    )(*[pltpu.with_memory_space_constraint(x, pltpu.HBM) for x in (margin_diag, coupling_near, coupling_far, leaf_factor, tile_rows, tile_counts)])


def solution(mesh):
    spec = jax.sharding.PartitionSpec
    return jax.shard_map(
        per_device,
        mesh=mesh,
        in_specs=(
            spec("leaf", "tile"),
            spec("leaf", "tile"),
            spec("leaf", "tile"),
            spec("leaf", "tile"),
            spec("leaf", None, None),
            spec("leaf", None),
        ),
        out_specs=spec(None, ("leaf", "tile")),
        check_vma=False,
    )
```

```python
import functools

import jax
import jax.numpy as jnp
from jax import lax
from jax.experimental import pallas as pl
from jax.experimental.pallas import tpu as pltpu

MESH = pl.DeviceIdType.MESH
T = 256
H = 128
Q = 64
KP = 136
F32 = jnp.float32
BF16 = jnp.bfloat16


def split(x):
    high = x.astype(BF16)
    return high, (x - high.astype(F32)).astype(BF16)


def nn(a, b):
    return lax.dot_general(a, b, (((1,), (0,)), ((), ())), preferred_element_type=F32)


def nt(a, b):
    return lax.dot_general(a, b, (((1,), (1,)), ((), ())), preferred_element_type=F32)


def mm(a, b, dot=nn):
    rows = a[0].shape[0]
    if rows <= 128:
        both = dot(jnp.concatenate([a[0], a[1]], 0), b[0])
        return both[:rows] + (both[rows:] + dot(a[0], b[1]))
    return dot(a[0], b[0]) + (dot(a[0], b[1]) + dot(a[1], b[0]))


def put(pair_ref, index, value):
    high, low = split(value)
    pair_ref[(0,) + index] = high
    pair_ref[(1,) + index] = low


def get(pair_ref, index):
    return pair_ref[(0,) + index], pair_ref[(1,) + index]


ALL = slice(None)


def tl(k):
    return slice(k * T, (k + 1) * T)


def eye(offset, rows):
    row = lax.broadcasted_iota(jnp.int32, (rows, T), 0) + offset
    col = lax.broadcasted_iota(jnp.int32, (rows, T), 1)
    return jnp.where(row == col, 1.0, 0.0).astype(F32)


def fold(block):
    row = lax.broadcasted_iota(jnp.int32, (Q, H), 0)
    col = lax.broadcasted_iota(jnp.int32, (Q, H), 1)
    top, low = block[:Q], block[Q:]
    inside = jnp.logical_and(col > row, col < Q)
    line = jnp.sum(jnp.where(col == row + Q, low, 0.0), axis=0, keepdims=True)
    return jnp.concatenate([jnp.where(inside, pltpu.roll(low, Q, 1), top), jnp.broadcast_to(line, (8, H))], axis=0)


def unfold(rows):
    row = lax.broadcasted_iota(jnp.int32, (Q, H), 0)
    col = lax.broadcasted_iota(jnp.int32, (Q, H), 1)
    top, line = rows[:Q], rows[Q:Q + 1]
    upper = jnp.where(jnp.logical_or(col < row, col >= Q), top, 0.0)
    lower = jnp.where(col > row + Q, pltpu.roll(top, Q, 1), 0.0)
    side = jnp.concatenate([upper, lower], axis=0)
    diagonal = jnp.concatenate([jnp.where(col == row, top, 0.0), jnp.where(col == row + Q, line, 0.0)], axis=0)
    return side + side.T + diagonal


def kernel(
    stride,
    diag_ref, near_ref, far_ref, leaf_ref, rows_ref, counts_ref,
    out_ref,
    zin, rows_s, counts_s, own_diag, c_raw, c_own, d_raw, uraw, packed, ncr, masks, mown,
    unit, pf, ff, fx, ut, a_mat, far_s, p_mat, q_mat, f_mat, f_cross,
    local, ssem, rsem,
):
    leaf = lax.axis_index("leaf")
    core = lax.axis_index("tile")
    pos = leaf // stride
    rest = leaf % stride
    pos1 = pos + 1 - 2 * (pos % 2)
    pos2 = (pos + 2) % 4
    pos3 = 3 - pos
    spot = (pos, pos1, pos2, pos3)
    dev1 = (pos1 * stride + rest, core)
    dev3 = (pos3 * stride + rest, core)
    mate = (leaf, 1 - core)
    half = pl.multiple_of(core * H, H)
    mine = pl.ds(half, H)
    away = pl.ds(pl.multiple_of(H - half, H), H)

    barrier = pltpu.get_barrier_semaphore()
    for device in (dev1, dev3, mate):
        pl.semaphore_signal(barrier, inc=1, device_id=device, device_id_type=MESH)

    loads = [
        pltpu.make_async_copy(a, b, local.at[i])
        for i, (a, b) in enumerate((
            (leaf_ref, zin), (near_ref, c_raw.at[0, core]), (diag_ref, own_diag.at[core]),
            (far_ref, d_raw.at[0, core]), (rows_ref, rows_s), (counts_ref, counts_s),
        ))
    ]
    for load in loads:
        load.start()

    copies = {}

    def plan(name, src, dst, device):
        index = len(copies)
        copies[name] = pltpu.make_async_remote_copy(
            src_ref=src, dst_ref=dst, send_sem=ssem.at[index], recv_sem=rsem.at[index],
            device_id=device, device_id_type=MESH,
        )

    def same(name, ref, device):
        plan(name, ref, ref, device)

    def start(*names):
        for name in names:
            copies[name].start()

    def arrived(*names):
        for name in names:
            copies[name].wait_recv()

    plan("C1", c_raw.at[0, core], c_raw.at[1, core], dev1)
    for key, buf, rows in (("U", uraw, (Q, Q)), ("K", packed, (KP - Q, Q)), ("D", d_raw, (H, H))):
        first, second = pl.ds(0, rows[0]), pl.ds(rows[0], rows[1])
        plan(key + "1b", buf.at[0, core, second], buf.at[1, core, second], dev1)
        plan(key + "1a", buf.at[0, core, first], buf.at[1, core, first], dev1)
        plan(key + "3a", buf.at[0, core, first], buf.at[3, core, first], dev3)
        plan(key + "3b", buf.at[0, core, second], buf.at[3, core, second], dev3)
        plan("f" + key + "1", buf.at[3, core, first], buf.at[2, core, first], dev1)
        plan("f" + key + "3", buf.at[1, core, second], buf.at[2, core, second], dev3)
        if key != "K":
            same("m" + key + "0", buf.at[0, core], mate)
        same("m" + key + "1", buf.at[1, core], mate)
        same("m" + key + "3", buf.at[3, core], mate)
        same("m" + key + "2a", buf.at[2, core, first], mate)
        same("m" + key + "2b", buf.at[2, core, second], mate)
    plan("mC0", c_raw.at[0, core, away], c_own.at[:], mate)
    same("mR", ncr.at[0, mine], mate)
    same("mG0", own_diag.at[core], mate)
    plan("N3", ncr.at[0, mine], ncr.at[1, mine], dev3)
    same("mN", ncr.at[1, mine], mate)
    plan("M1", mown, masks.at[1], dev1)
    plan("M3", mown, masks.at[3], dev3)
    plan("fM1", masks.at[3], masks.at[2], dev1)
    for g in range(2):
        for r in range(2):
            same("xP%d%d" % (g, r), pf.at[g, core, r], mate)
    for g in range(2):
        same("xF%d" % g, ff.at[g, core], mate)
    same("xX", fx.at[core], mate)

    loads[4].wait()
    loads[5].wait()
    for level in range(2):
        for s in range(4):
            hit = jnp.float32(0.0)
            for e in range(4):
                value = rows_s[0, level, e]
                place = 2 * (value // (2 * stride) % 2) + value // stride % 2
                live = jnp.logical_and(e < counts_s[0, level], place == spot[s])
                hit = jnp.where(live, jnp.float32(1.0), hit)
            mown[level * 4 + s:level * 4 + s + 1, :] = jnp.full((1, 128), hit, F32)
    masks[0] = mown[...]

    unit[0, :, :T] = 1.5 * eye(0, T)
    unit[0, :, T:] = jnp.zeros((T, T), F32)
    unit[1, :, :T] = jnp.zeros((T, T), F32)
    unit[1, :, T:] = 1.5 * eye(0, T)
    loads[0].wait()
    uraw[0, core] = zin[...].T
    loads[1].wait()
    pl.semaphore_wait(barrier, 3)
    start("M1", "M3", "C1", "U3a", "U3b", "U1b", "U1a", "mC0", "mU0")
    loads[2].wait()
    top = own_diag[core, mine]
    packed[0, core, 0:KP - Q] = fold(top)
    other = own_diag[core, away]
    other = jnp.where(core == 0, other, other.T)
    packed[0, core, KP - Q:KP] = jnp.where(core == 0, other[:Q], other[Q:])
    start("K3a", "K3b", "K1b", "K1a", "mG0")
    loads[3].wait()
    start("mD0")
    def mask(level, column, row):
        line = masks[column, level * 4 + (column ^ row):level * 4 + (column ^ row) + 1, :]
        return jnp.concatenate([line, line], axis=1)

    def wide(line):
        return jnp.concatenate([line, line], axis=1)

    def whole(ref, slot):
        return jnp.concatenate([ref[slot, 0], ref[slot, 1]], axis=1)

    def put_near(g, cross):
        first, second = (0, 1) if g == 0 else (1, 0)
        put(a_mat, (g, tl(first), tl(second)), cross)
        put(a_mat, (g, tl(second), tl(first)), cross.T)

    def put_diag(slot):
        g, k = slot // 2, slot % 2
        low, high = packed[slot, 0], packed[slot, 1]
        below = jnp.concatenate([low[KP - Q:], high[KP - Q:]], axis=0)
        full = jnp.concatenate([
            jnp.concatenate([unfold(low), below.T], axis=1),
            jnp.concatenate([below, unfold(high)], axis=1),
        ], axis=0)
        put(a_mat, (g, tl(k), tl(k)), -0.5 * full)

    def put_leaf(slot):
        put(ut, (slot,), jnp.concatenate([uraw[slot, 0], uraw[slot, 1]], axis=0))

    own_rows = pl.ds(pl.multiple_of(core * T, T), T)
    mate_rows = pl.ds(pl.multiple_of(T - core * T, T), T)

    def sweep1(g, *places):
        hold = {}

        def one():
            for j, r in places:
                hold[j, r] = split(mm(get(ut, (2 * g + j,)), get(a_mat, (g, tl(j), tl(r)))))

        def two():
            for j, r in places:
                f = mm(hold[j, r], get(ut, (2 * g + r,)), nt)
                hold[j, r] = split(f + unit[0, :, :T] if r == j else f)

        def three():
            for j, r in places:
                new = mm(hold[j, r], get(ut, (2 * g + r,)))
                put(p_mat, (g, tl(j), tl(r)), new * mask(0, 2 * g + j, 2 * g + r))

        return one, two, three

    def newton(gram):
        return gram + unit[core]

    def sweep2(g):
        hold = []

        def one():
            hold.append(split(mm(get(p_mat, (g, own_rows)), get(a_mat, (g,)))))

        def two():
            hold.append(split(newton(mm(hold[0], get(p_mat, (g,)), nt))))

        def three():
            for r in range(2):
                line = masks[2 * g + core, pl.ds(core if r == 0 else 1 - core, 1), :]
                new = mm(hold[1], get(p_mat, (g, ALL, tl(r)))) * wide(line)
                pf[g, core, r] = new
                put(q_mat, (g, own_rows, tl(r)), new)
            start("xP%d0" % g, "xP%d1" % g)

        return one, two, three

    def join(g):
        for r in range(2):
            put(q_mat, (g, mate_rows, tl(r)), pf[g, 1 - core, r])

    def gram1(g):
        hold = []

        def one():
            hold.append(split(mm(get(q_mat, (g, own_rows)), get(a_mat, (g,)))))

        def two():
            f = newton(mm(hold[0], get(q_mat, (g,)), nt))
            ff[g, core] = f
            start("xF%d" % g)
            put(f_mat, (g, own_rows), f)

        return one, two

    def fin(g):
        put(f_mat, (g, mate_rows), ff[g, 1 - core])

    def run(*steps):
        for step in steps:
            step()

    arrived("mC0", "C1")
    mixed = c_raw[0, core, mine]
    rows = jnp.where(core == 0, jnp.concatenate([mixed, c_own[...]], axis=1), jnp.concatenate([c_own[...], mixed], axis=1))
    ncr[0, mine] = -0.25 * (rows + c_raw[1, core].T)
    start("N3", "mR")
    arrived("M3")
    start("fM1")
    arrived("U3a")
    start("fU1")
    arrived("U3b")
    start("mU3")
    arrived("K3a")
    start("fK1", "D1b", "D1a")
    arrived("U1b")
    start("fU3")
    arrived("mG0", "mU0", "mR", "M1")
    put(a_mat, (0, tl(0), tl(0)), -0.5 * jnp.concatenate([own_diag[0], own_diag[1]], axis=1))
    put_leaf(0)
    put_near(0, ncr[0])
    run(*sweep1(0, (0, 0)))
    arrived("U1a", "K3b")
    start("mU1", "mK3")
    arrived("K1b")
    start("fK3", "D3a", "D3b")
    arrived("mU1")
    put_leaf(1)
    a = sweep1(0, (0, 1), (1, 0))
    run(a[0])
    arrived("K1a", "mU3", "mK3")
    start("mK1")
    put_leaf(3)
    put_diag(3)
    run(*a[1:])
    b = sweep1(1, (1, 1))
    run(b[0])
    arrived("fM1", "N3", "mK1", "fU1")
    start("mN", "mU2a")
    put_diag(1)
    a = sweep1(0, (1, 1))
    run(a[0], b[1], a[1], b[2], a[2])
    arrived("fU3", "fK1")
    start("mU2b", "mK2a")
    a = sweep2(0)
    run(a[0], a[1])
    arrived("fK3", "mN", "mU2a", "mU2b")
    start("mK2b")
    put_near(1, ncr[1])
    put_leaf(2)
    b = sweep1(1, (0, 1), (1, 0))
    run(a[2])
    arrived("D1b", "D3a")
    start("fD3", "fD1")
    run(*b)
    arrived("mK2a", "mK2b")
    put_diag(2)
    run(*sweep1(1, (0, 0)))
    arrived("D1a", "D3b")
    start("mD1", "mD3")
    run(*sweep2(1))
    arrived("xP00", "xP01")
    join(0)
    a = gram1(0)
    run(a[0])
    arrived("mD1", "mD3", "fD1", "fD3")
    start("mD2a", "mD2b")
    put(far_s, (1,), -0.25 * (whole(d_raw, 1) + whole(d_raw, 3).T))
    run(a[1])
    arrived("xP10", "xP11")
    join(1)
    run(*gram1(1))
    arrived("xF0", "mD0", "mD2a", "mD2b")
    fin(0)
    u0 = mm(get(f_mat, (0, mine, ALL)), get(q_mat, (0,)))
    put(far_s, (0,), -0.25 * (whole(d_raw, 0) + whole(d_raw, 2).T))

    second = pl.ds(pl.multiple_of(T + half, H), H)
    v = []
    for k in range(2):
        rows = tuple(
            jnp.concatenate([q_mat[i, 0, mine, tl(k)], q_mat[i, 0, second, tl(k)]], axis=0)
            for i in range(2)
        )
        v.append(mm(rows, get(far_s, (k,))))
    f = mm(split(jnp.concatenate(v, axis=1)), get(q_mat, (1,)), nt)
    fx[core] = f
    start("xX")
    f = split(f)
    for i in range(2):
        f_cross[i, mine] = f[i][:H]
        f_cross[i, second] = f[i][H:]
    u1 = mm((f[0][:H], f[1][:H]), get(q_mat, (1,)))
    u = [u0[:, tl(0)], u0[:, tl(1)], u1[:, tl(0)], u1[:, tl(1)]]
    u = [u[r] * mask(1, 0, r) for r in range(4)]
    us = [split(x) for x in u]

    def beside(parts):
        return tuple(jnp.concatenate([part[i] for part in parts], axis=1) for i in range(2))

    v = []
    for g in range(2):
        vg = mm(beside(us[2 * g:2 * g + 2]), get(a_mat, (g,)))
        for k in range(2):
            extra = mm(us[2 - 2 * g + k], get(far_s, (k,)), nn if g == 1 else nt)
            v.append(split(vg[:, tl(k)] + extra))
    ga = [mm(v[r], get(q_mat, (r // 2, ALL, tl(r % 2))), nt) for r in range(4)]
    arrived("xF1", "xX")
    fin(1)
    f = split(fx[1 - core])
    for i in range(2):
        f_cross[i, away] = f[i][:H]
        f_cross[i, pl.ds(pl.multiple_of(T + H - half, H), H)] = f[i][H:]
    ds = []
    for l in range(4):
        lhs = []
        for g in range(2):
            m0, m1 = wide(mask(1, l, 2 * g)), wide(mask(1, l, 2 * g + 1))
            lhs.append(split(m0 * ga[2 * g] + m1 * ga[2 * g + 1]))
        k = l % 2
        if l < 2:
            gram = mm(lhs[0], get(f_mat, (0, ALL, tl(k)))) + mm(lhs[1], get(f_cross, (tl(k), ALL)), nt)
        else:
            gram = mm(lhs[0], get(f_cross, (ALL, tl(k)))) + mm(lhs[1], get(f_mat, (1, ALL, tl(k))))
        ds.append(split(gram + 0.5 * eye(half, H) if l == 0 else gram))
    terms = [[], []]
    for l in range(4):
        k = l % 2
        if l < 2:
            terms[0].append(mm(ds[l], get(f_mat, (0, tl(k), ALL))))
            terms[1].append(mm(ds[l], get(f_cross, (tl(k), ALL))))
        else:
            terms[0].append(mm(ds[l], get(f_cross, (ALL, tl(k))), nt))
            terms[1].append(mm(ds[l], get(f_mat, (1, tl(k), ALL))))
    for r in range(4):
        g, k = r // 2, r % 2
        x = 0.0
        for l in range(4):
            x = x + wide(mask(1, l, r)) * terms[g][l]
        last = u[r] + mm(split(x), get(q_mat, (g, ALL, tl(k))))
        last = last * mask(1, 0, r)
        out_ref[pl.ds(pl.multiple_of(spot[r] * T, T), T), :] = last.T

    for copy in copies.values():
        copy.wait_send()


def per_device(margin_diag, coupling_near, coupling_far, leaf_factor, tile_rows, tile_counts):
    stride = lax.axis_size("leaf") // 4
    vmem = pl.BlockSpec(memory_space=pltpu.VMEM)
    hbm = pl.BlockSpec(memory_space=pl.ANY)
    dma = pltpu.SemaphoreType.DMA
    return pl.pallas_call(
        functools.partial(kernel, stride),
        out_shape=jax.ShapeDtypeStruct((4 * T, H), F32),
        in_specs=[hbm] * 6,
        out_specs=vmem,
        scratch_shapes=[
            pltpu.VMEM((T, H), F32),
            pltpu.SMEM((1, 2, 4), jnp.int32),
            pltpu.SMEM((1, 2), jnp.int32),
            pltpu.VMEM((2, T, H), F32),
            pltpu.VMEM((2, 2, T, H), F32),
            pltpu.VMEM((H, H), F32),
            pltpu.VMEM((4, 2, T, H), F32),
            pltpu.VMEM((4, 2, H, T), F32),
            pltpu.VMEM((4, 2, KP, H), F32),
            pltpu.VMEM((2, T, T), F32),
            pltpu.VMEM((4, 8, 128), F32),
            pltpu.VMEM((8, 128), F32),
            pltpu.VMEM((2, T, 2 * T), F32),
            pltpu.VMEM((2, 2, 2, T, T), F32),
            pltpu.VMEM((2, 2, T, 2 * T), F32),
            pltpu.VMEM((2, T, 2 * T), F32),
            pltpu.VMEM((2, 4, T, T), BF16),
            pltpu.VMEM((2, 2, 2 * T, 2 * T), BF16),
            pltpu.VMEM((2, 2, T, T), BF16),
            pltpu.VMEM((2, 2, 2 * T, 2 * T), BF16),
            pltpu.VMEM((2, 2, 2 * T, 2 * T), BF16),
            pltpu.VMEM((2, 2, 2 * T, 2 * T), BF16),
            pltpu.VMEM((2, 2 * T, 2 * T), BF16),
            dma((6,)), dma((64,)), dma((64,)),
        ],
        compiler_params=pltpu.CompilerParams(
            collective_id=0, has_side_effects=True, vmem_limit_bytes=50 * 2**20
        ),
    )(*[pltpu.with_memory_space_constraint(x, pltpu.HBM) for x in (margin_diag, coupling_near, coupling_far, leaf_factor, tile_rows, tile_counts)])


def solution(mesh):
    spec = jax.sharding.PartitionSpec
    return jax.shard_map(
        per_device,
        mesh=mesh,
        in_specs=(
            spec("leaf", "tile"),
            spec("leaf", "tile"),
            spec("leaf", "tile"),
            spec("leaf", "tile"),
            spec("leaf", None, None),
            spec("leaf", None),
        ),
        out_specs=spec(None, ("leaf", "tile")),
        check_vma=False,
    )
```

```python
import functools

import jax
import jax.numpy as jnp
from jax import lax
from jax.experimental import pallas as pl
from jax.experimental.pallas import tpu as pltpu

MESH = pl.DeviceIdType.MESH
T = 256
H = 128
Q = 64
KP = 136
F32 = jnp.float32
BF16 = jnp.bfloat16


def split(x):
    high = x.astype(BF16)
    return high, (x - high.astype(F32)).astype(BF16)


def nn(a, b):
    return lax.dot_general(a, b, (((1,), (0,)), ((), ())), preferred_element_type=F32)


def nt(a, b):
    return lax.dot_general(a, b, (((1,), (1,)), ((), ())), preferred_element_type=F32)


def mm(a, b, dot=nn):
    rows = a[0].shape[0]
    if rows <= 128:
        both = dot(jnp.concatenate([a[0], a[1]], 0), b[0])
        return both[:rows] + (both[rows:] + dot(a[0], b[1]))
    return dot(a[0], b[0]) + (dot(a[0], b[1]) + dot(a[1], b[0]))


def put(pair_ref, index, value):
    high, low = split(value)
    pair_ref[(0,) + index] = high
    pair_ref[(1,) + index] = low


def get(pair_ref, index):
    return pair_ref[(0,) + index], pair_ref[(1,) + index]


ALL = slice(None)


def tl(k):
    return slice(k * T, (k + 1) * T)


def eye(offset, rows):
    row = lax.broadcasted_iota(jnp.int32, (rows, T), 0) + offset
    col = lax.broadcasted_iota(jnp.int32, (rows, T), 1)
    return jnp.where(row == col, 1.0, 0.0).astype(F32)


def fold(block):
    row = lax.broadcasted_iota(jnp.int32, (Q, H), 0)
    col = lax.broadcasted_iota(jnp.int32, (Q, H), 1)
    top, low = block[:Q], block[Q:]
    inside = jnp.logical_and(col > row, col < Q)
    line = jnp.sum(jnp.where(col == row + Q, low, 0.0), axis=0, keepdims=True)
    return jnp.concatenate([jnp.where(inside, pltpu.roll(low, Q, 1), top), jnp.broadcast_to(line, (8, H))], axis=0)


def unfold(rows):
    row = lax.broadcasted_iota(jnp.int32, (Q, H), 0)
    col = lax.broadcasted_iota(jnp.int32, (Q, H), 1)
    top, line = rows[:Q], rows[Q:Q + 1]
    upper = jnp.where(jnp.logical_or(col < row, col >= Q), top, 0.0)
    lower = jnp.where(col > row + Q, pltpu.roll(top, Q, 1), 0.0)
    side = jnp.concatenate([upper, lower], axis=0)
    diagonal = jnp.concatenate([jnp.where(col == row, top, 0.0), jnp.where(col == row + Q, line, 0.0)], axis=0)
    return side + side.T + diagonal


def kernel(
    stride,
    diag_ref, near_ref, far_ref, leaf_ref, rows_ref, counts_ref,
    out_ref,
    zin, rows_s, counts_s, own_diag, c_raw, c_own, d_raw, uraw, packed, ncr, masks, mown,
    unit, pf, ff, fx, ut, a_mat, far_s, p_mat, q_mat, f_mat, f_cross,
    local, ssem, rsem,
):
    leaf = lax.axis_index("leaf")
    core = lax.axis_index("tile")
    pos = leaf // stride
    rest = leaf % stride
    pos1 = pos + 1 - 2 * (pos % 2)
    pos2 = (pos + 2) % 4
    pos3 = 3 - pos
    spot = (pos, pos1, pos2, pos3)
    dev1 = (pos1 * stride + rest, core)
    dev3 = (pos3 * stride + rest, core)
    mate = (leaf, 1 - core)
    half = pl.multiple_of(core * H, H)
    mine = pl.ds(half, H)
    away = pl.ds(pl.multiple_of(H - half, H), H)

    barrier = pltpu.get_barrier_semaphore()
    for device in (dev1, dev3, mate):
        pl.semaphore_signal(barrier, inc=1, device_id=device, device_id_type=MESH)

    loads = [
        pltpu.make_async_copy(a, b, local.at[i])
        for i, (a, b) in enumerate((
            (leaf_ref, zin), (near_ref, c_raw.at[0, core]), (diag_ref, own_diag.at[core]),
            (far_ref, d_raw.at[0, core]), (rows_ref, rows_s), (counts_ref, counts_s),
        ))
    ]
    for load in loads:
        load.start()

    copies = {}

    def plan(name, src, dst, device):
        index = len(copies)
        copies[name] = pltpu.make_async_remote_copy(
            src_ref=src, dst_ref=dst, send_sem=ssem.at[index], recv_sem=rsem.at[index],
            device_id=device, device_id_type=MESH,
        )

    def same(name, ref, device):
        plan(name, ref, ref, device)

    def start(*names):
        for name in names:
            copies[name].start()

    def arrived(*names):
        for name in names:
            copies[name].wait_recv()

    plan("C1", c_raw.at[0, core], c_raw.at[1, core], dev1)
    for key, buf, rows in (("U", uraw, (Q, Q)), ("K", packed, (KP - Q, Q)), ("D", d_raw, (H, H))):
        first, second = pl.ds(0, rows[0]), pl.ds(rows[0], rows[1])
        plan(key + "1b", buf.at[0, core, second], buf.at[1, core, second], dev1)
        plan(key + "1a", buf.at[0, core, first], buf.at[1, core, first], dev1)
        plan(key + "3a", buf.at[0, core, first], buf.at[3, core, first], dev3)
        plan(key + "3b", buf.at[0, core, second], buf.at[3, core, second], dev3)
        plan("f" + key + "1", buf.at[3, core, first], buf.at[2, core, first], dev1)
        plan("f" + key + "3", buf.at[1, core, second], buf.at[2, core, second], dev3)
        if key != "K":
            same("m" + key + "0", buf.at[0, core], mate)
        same("m" + key + "1", buf.at[1, core], mate)
        same("m" + key + "3", buf.at[3, core], mate)
        same("m" + key + "2a", buf.at[2, core, first], mate)
        same("m" + key + "2b", buf.at[2, core, second], mate)
    plan("mC0", c_raw.at[0, core, away], c_own.at[:], mate)
    same("mR", ncr.at[0, mine], mate)
    same("mG0", own_diag.at[core], mate)
    plan("N3", ncr.at[0, mine], ncr.at[1, mine], dev3)
    same("mN", ncr.at[1, mine], mate)
    plan("M1", mown, masks.at[1], dev1)
    plan("M3", mown, masks.at[3], dev3)
    plan("fM1", masks.at[3], masks.at[2], dev1)
    for g in range(2):
        for r in range(2):
            same("xP%d%d" % (g, r), pf.at[g, core, r], mate)
    for g in range(2):
        same("xF%d" % g, ff.at[g, core], mate)
    same("xX", fx.at[core], mate)

    loads[4].wait()
    loads[5].wait()
    for level in range(2):
        for s in range(4):
            hit = jnp.float32(0.0)
            for e in range(4):
                value = rows_s[0, level, e]
                place = 2 * (value // (2 * stride) % 2) + value // stride % 2
                live = jnp.logical_and(e < counts_s[0, level], place == spot[s])
                hit = jnp.where(live, jnp.float32(1.0), hit)
            mown[level * 4 + s:level * 4 + s + 1, :] = jnp.full((1, 128), hit, F32)
    masks[0] = mown[...]

    unit[0, :, :T] = 1.5 * eye(0, T)
    unit[0, :, T:] = jnp.zeros((T, T), F32)
    unit[1, :, :T] = jnp.zeros((T, T), F32)
    unit[1, :, T:] = 1.5 * eye(0, T)
    loads[0].wait()
    uraw[0, core] = zin[...].T
    loads[1].wait()
    pl.semaphore_wait(barrier, 3)
    start("M1", "M3", "C1", "U3a", "U3b", "U1b", "U1a", "mC0", "mU0")
    loads[2].wait()
    top = own_diag[core, mine]
    packed[0, core, 0:KP - Q] = fold(top)
    other = own_diag[core, away]
    other = jnp.where(core == 0, other, other.T)
    packed[0, core, KP - Q:KP] = jnp.where(core == 0, other[:Q], other[Q:])
    start("K3a", "K3b", "K1b", "K1a", "mG0")
    loads[3].wait()
    start("mD0")
    def mask(level, column, row):
        line = masks[column, level * 4 + (column ^ row):level * 4 + (column ^ row) + 1, :]
        return jnp.concatenate([line, line], axis=1)

    def wide(line):
        return jnp.concatenate([line, line], axis=1)

    def whole(ref, slot):
        return jnp.concatenate([ref[slot, 0], ref[slot, 1]], axis=1)

    def put_near(g, cross):
        first, second = (0, 1) if g == 0 else (1, 0)
        put(a_mat, (g, tl(first), tl(second)), cross)
        put(a_mat, (g, tl(second), tl(first)), cross.T)

    def put_diag(slot):
        g, k = slot // 2, slot % 2
        low, high = packed[slot, 0], packed[slot, 1]
        below = jnp.concatenate([low[KP - Q:], high[KP - Q:]], axis=0)
        full = jnp.concatenate([
            jnp.concatenate([unfold(low), below.T], axis=1),
            jnp.concatenate([below, unfold(high)], axis=1),
        ], axis=0)
        put(a_mat, (g, tl(k), tl(k)), -0.5 * full)

    def put_leaf(slot):
        put(ut, (slot,), jnp.concatenate([uraw[slot, 0], uraw[slot, 1]], axis=0))

    own_rows = pl.ds(pl.multiple_of(core * T, T), T)
    mate_rows = pl.ds(pl.multiple_of(T - core * T, T), T)

    def sweep1(g, *places):
        hold = {}

        def one():
            for j, r in places:
                hold[j, r] = split(mm(get(ut, (2 * g + j,)), get(a_mat, (g, tl(j), tl(r)))))

        def two():
            for j, r in places:
                f = mm(hold[j, r], get(ut, (2 * g + r,)), nt)
                hold[j, r] = split(f + unit[0, :, :T] if r == j else f)

        def three():
            for j, r in places:
                new = mm(hold[j, r], get(ut, (2 * g + r,)))
                put(p_mat, (g, tl(j), tl(r)), new * mask(0, 2 * g + j, 2 * g + r))

        return one, two, three

    def newton(gram):
        return gram + unit[core]

    def sweep2(g):
        hold = []

        def one():
            hold.append(split(mm(get(p_mat, (g, own_rows)), get(a_mat, (g,)))))

        def two():
            hold.append(split(newton(mm(hold[0], get(p_mat, (g,)), nt))))

        def three():
            for r in range(2):
                line = masks[2 * g + core, pl.ds(core if r == 0 else 1 - core, 1), :]
                new = mm(hold[1], get(p_mat, (g, ALL, tl(r)))) * wide(line)
                pf[g, core, r] = new
                put(q_mat, (g, own_rows, tl(r)), new)
            start("xP%d0" % g, "xP%d1" % g)

        return one, two, three

    def join(g):
        for r in range(2):
            put(q_mat, (g, mate_rows, tl(r)), pf[g, 1 - core, r])

    def gram1(g):
        hold = []

        def one():
            hold.append(split(mm(get(q_mat, (g, own_rows)), get(a_mat, (g,)))))

        def two():
            f = newton(mm(hold[0], get(q_mat, (g,)), nt))
            ff[g, core] = f
            start("xF%d" % g)
            put(f_mat, (g, own_rows), f)

        return one, two

    def fin(g):
        put(f_mat, (g, mate_rows), ff[g, 1 - core])

    def run(*steps):
        for step in steps:
            step()

    arrived("mC0", "C1")
    mixed = c_raw[0, core, mine]
    rows = jnp.where(core == 0, jnp.concatenate([mixed, c_own[...]], axis=1), jnp.concatenate([c_own[...], mixed], axis=1))
    ncr[0, mine] = -0.25 * (rows + c_raw[1, core].T)
    start("N3", "mR")
    arrived("M3")
    start("fM1")
    arrived("U3a")
    start("fU1")
    arrived("U3b")
    start("mU3")
    arrived("K3a")
    start("fK1", "D1b", "D1a")
    arrived("U1b")
    start("fU3")
    arrived("mG0", "mU0", "mR", "M1")
    put(a_mat, (0, tl(0), tl(0)), -0.5 * jnp.concatenate([own_diag[0], own_diag[1]], axis=1))
    put_leaf(0)
    put_near(0, ncr[0])
    run(*sweep1(0, (0, 0)))
    arrived("U1a", "K3b")
    start("mU1", "mK3")
    arrived("K1b")
    start("fK3", "D3a", "D3b")
    arrived("mU1")
    put_leaf(1)
    a = sweep1(0, (0, 1), (1, 0))
    run(a[0])
    arrived("K1a", "mU3", "mK3")
    start("mK1")
    put_leaf(3)
    put_diag(3)
    run(*a[1:])
    b = sweep1(1, (1, 1))
    run(b[0])
    arrived("fM1", "N3", "mK1", "fU1")
    start("mN", "mU2a")
    put_diag(1)
    a = sweep1(0, (1, 1))
    run(a[0], b[1], a[1], b[2], a[2])
    arrived("fU3", "fK1")
    start("mU2b", "mK2a")
    a = sweep2(0)
    run(a[0], a[1])
    arrived("fK3")
    start("mK2b")
    run(a[2])
    arrived("mN", "mU2a", "mU2b", "D1b", "D3a")
    start("fD3", "fD1")
    put_near(1, ncr[1])
    put_leaf(2)
    b = sweep1(1, (0, 1), (1, 0))
    run(b[0])
    arrived("mK2a", "mK2b")
    put_diag(2)
    c = sweep1(1, (0, 0))
    run(b[1], c[0], b[2], c[1], c[2])
    arrived("D1a", "D3b")
    start("mD1", "mD3")
    run(*sweep2(1))
    arrived("xP00", "xP01")
    join(0)
    a = gram1(0)
    run(a[0])
    arrived("mD1", "mD3", "fD1", "fD3")
    start("mD2a", "mD2b")
    put(far_s, (1,), -0.25 * (whole(d_raw, 1) + whole(d_raw, 3).T))
    run(a[1])
    arrived("xP10", "xP11")
    join(1)
    run(*gram1(1))
    arrived("xF0", "mD0", "mD2a", "mD2b")
    fin(0)
    u0 = mm(get(f_mat, (0, mine, ALL)), get(q_mat, (0,)))
    put(far_s, (0,), -0.25 * (whole(d_raw, 0) + whole(d_raw, 2).T))

    second = pl.ds(pl.multiple_of(T + half, H), H)
    v = []
    for k in range(2):
        rows = tuple(
            jnp.concatenate([q_mat[i, 0, mine, tl(k)], q_mat[i, 0, second, tl(k)]], axis=0)
            for i in range(2)
        )
        v.append(mm(rows, get(far_s, (k,))))
    f = mm(split(jnp.concatenate(v, axis=1)), get(q_mat, (1,)), nt)
    fx[core] = f
    start("xX")
    f = split(f)
    for i in range(2):
        f_cross[i, mine] = f[i][:H]
        f_cross[i, second] = f[i][H:]
    u1 = mm((f[0][:H], f[1][:H]), get(q_mat, (1,)))
    u = [u0[:, tl(0)], u0[:, tl(1)], u1[:, tl(0)], u1[:, tl(1)]]
    u = [u[r] * mask(1, 0, r) for r in range(4)]
    us = [split(x) for x in u]

    def beside(parts):
        return tuple(jnp.concatenate([part[i] for part in parts], axis=1) for i in range(2))

    v = []
    for g in range(2):
        vg = mm(beside(us[2 * g:2 * g + 2]), get(a_mat, (g,)))
        for k in range(2):
            extra = mm(us[2 - 2 * g + k], get(far_s, (k,)), nn if g == 1 else nt)
            v.append(split(vg[:, tl(k)] + extra))
    ga = [mm(v[r], get(q_mat, (r // 2, ALL, tl(r % 2))), nt) for r in range(4)]
    arrived("xF1", "xX")
    fin(1)
    f = split(fx[1 - core])
    for i in range(2):
        f_cross[i, away] = f[i][:H]
        f_cross[i, pl.ds(pl.multiple_of(T + H - half, H), H)] = f[i][H:]
    ds = []
    for l in range(4):
        lhs = []
        for g in range(2):
            m0, m1 = wide(mask(1, l, 2 * g)), wide(mask(1, l, 2 * g + 1))
            lhs.append(split(m0 * ga[2 * g] + m1 * ga[2 * g + 1]))
        k = l % 2
        if l < 2:
            gram = mm(lhs[0], get(f_mat, (0, ALL, tl(k)))) + mm(lhs[1], get(f_cross, (tl(k), ALL)), nt)
        else:
            gram = mm(lhs[0], get(f_cross, (ALL, tl(k)))) + mm(lhs[1], get(f_mat, (1, ALL, tl(k))))
        ds.append(split(gram + 0.5 * eye(half, H) if l == 0 else gram))
    terms = [[], []]
    for l in range(4):
        k = l % 2
        if l < 2:
            terms[0].append(mm(ds[l], get(f_mat, (0, tl(k), ALL))))
            terms[1].append(mm(ds[l], get(f_cross, (tl(k), ALL))))
        else:
            terms[0].append(mm(ds[l], get(f_cross, (ALL, tl(k))), nt))
            terms[1].append(mm(ds[l], get(f_mat, (1, tl(k), ALL))))
    for r in range(4):
        g, k = r // 2, r % 2
        x = 0.0
        for l in range(4):
            x = x + wide(mask(1, l, r)) * terms[g][l]
        last = u[r] + mm(split(x), get(q_mat, (g, ALL, tl(k))))
        last = last * mask(1, 0, r)
        out_ref[pl.ds(pl.multiple_of(spot[r] * T, T), T), :] = last.T

    for copy in copies.values():
        copy.wait_send()


def per_device(margin_diag, coupling_near, coupling_far, leaf_factor, tile_rows, tile_counts):
    stride = lax.axis_size("leaf") // 4
    vmem = pl.BlockSpec(memory_space=pltpu.VMEM)
    hbm = pl.BlockSpec(memory_space=pl.ANY)
    dma = pltpu.SemaphoreType.DMA
    return pl.pallas_call(
        functools.partial(kernel, stride),
        out_shape=jax.ShapeDtypeStruct((4 * T, H), F32),
        in_specs=[hbm] * 6,
        out_specs=vmem,
        scratch_shapes=[
            pltpu.VMEM((T, H), F32),
            pltpu.SMEM((1, 2, 4), jnp.int32),
            pltpu.SMEM((1, 2), jnp.int32),
            pltpu.VMEM((2, T, H), F32),
            pltpu.VMEM((2, 2, T, H), F32),
            pltpu.VMEM((H, H), F32),
            pltpu.VMEM((4, 2, T, H), F32),
            pltpu.VMEM((4, 2, H, T), F32),
            pltpu.VMEM((4, 2, KP, H), F32),
            pltpu.VMEM((2, T, T), F32),
            pltpu.VMEM((4, 8, 128), F32),
            pltpu.VMEM((8, 128), F32),
            pltpu.VMEM((2, T, 2 * T), F32),
            pltpu.VMEM((2, 2, 2, T, T), F32),
            pltpu.VMEM((2, 2, T, 2 * T), F32),
            pltpu.VMEM((2, T, 2 * T), F32),
            pltpu.VMEM((2, 4, T, T), BF16),
            pltpu.VMEM((2, 2, 2 * T, 2 * T), BF16),
            pltpu.VMEM((2, 2, T, T), BF16),
            pltpu.VMEM((2, 2, 2 * T, 2 * T), BF16),
            pltpu.VMEM((2, 2, 2 * T, 2 * T), BF16),
            pltpu.VMEM((2, 2, 2 * T, 2 * T), BF16),
            pltpu.VMEM((2, 2 * T, 2 * T), BF16),
            dma((6,)), dma((64,)), dma((64,)),
        ],
        compiler_params=pltpu.CompilerParams(
            collective_id=0, has_side_effects=True, vmem_limit_bytes=50 * 2**20
        ),
    )(*[pltpu.with_memory_space_constraint(x, pltpu.HBM) for x in (margin_diag, coupling_near, coupling_far, leaf_factor, tile_rows, tile_counts)])


def solution(mesh):
    spec = jax.sharding.PartitionSpec
    return jax.shard_map(
        per_device,
        mesh=mesh,
        in_specs=(
            spec("leaf", "tile"),
            spec("leaf", "tile"),
            spec("leaf", "tile"),
            spec("leaf", "tile"),
            spec("leaf", None, None),
            spec("leaf", None),
        ),
        out_specs=spec(None, ("leaf", "tile")),
        check_vma=False,
    )
```
